32 devices in a mesh: grp: 2 (over y), dom: 4 (over z), lvl: 2 (over x), sub: 2 (over core).
Axes of the slice: x: 2, y: 2, z: 4, core: 2. Of those that a mesh axis runs over, the one named last changes fastest.
Arguments:
- node_latents: bfloat16 [24576, 512], P(('grp', 'dom', 'lvl', 'sub')), parts along dimension 0, may hold values from -6 to 6
- coarse_latents: bfloat16 [2048, 512], P(('grp', 'dom', 'lvl', 'sub')), parts along dimension 0, may hold values from -6 to 6
- cotangent: bfloat16 [24576, 512], P(('grp', 'dom', 'lvl', 'sub')), parts along dimension 0, may hold values from -6 to 6
- w_message: bfloat16 [512, 512], replicated, may hold values from -0.25 to 0.25
- w_coarse: bfloat16 [512, 512], replicated, may hold values from -0.25 to 0.25
- w_update: bfloat16 [512, 512], replicated, may hold values from -0.25 to 0.25
- mask_words: int32 [24576, 8], P(('grp', 'dom', 'lvl', 'sub')), parts along dimension 0, may hold values from 0 to 65535
- tile_index: int32 [96, 16], P(('grp', 'dom', 'lvl', 'sub')), parts along dimension 0, may hold values from 0 to 767
- partner: int32 [6, 4], P('grp'), parts along dimension 0, may hold values from 0 to 3, as said below
- assignment: int32 [24576], P(('grp', 'dom', 'lvl', 'sub')), parts along dimension 0, may hold values from 0 to 127
- live_counts: int32 [32], P(('grp', 'dom', 'lvl', 'sub')), parts along dimension 0, may hold values from 192 to 768
Outputs:
- updated: bfloat16 [24576, 512], P(('grp', 'dom', 'lvl', 'sub')), parts along dimension 0
- d_nodes: bfloat16 [24576, 512], P(('grp', 'dom', 'lvl', 'sub')), parts along dimension 0
- d_coarse: bfloat16 [2048, 512], P(('grp', 'dom', 'lvl', 'sub')), parts along dimension 0
The draws below stay inside these ranges and needn't reach their ends.
There are 2 independent parts, one for each index of `grp`. The reference program is written for one: setup_inputs(seed, part) draws one part's arguments, and reference() takes and returns one part's arrays. A program takes and returns all parts, laid end to end along the dimension named above; an argument that names none is the same for every part. Nothing has to cross between parts.
Inputs may be any that keep to these rules, and one draw needn't show every extreme that they name: In each of the 3 rounds partner of partner is the part itself; a part may be its own partner in at most one round, and then its tile rows receive its own tile; a part's partners in different rounds all differ.
All inputs are finite; a program needn't handle non-finite values.
Results may differ from the reference program's by a relative error of at most 0.0071.
Values may be sent and summed in bfloat16 or wider, within the bound.
A program may use at most 64 MiB of HBM per device.

```python
import jax
import jax.numpy as jnp
import numpy as np

H = 512
NODE_DEV = 768
CD = 64
BT = 16
ROUNDS = 3
PIECES = 16
NODES = 12288
COARSE = 1024
GROUP_ROWS = 128
N_DOM = 4
N_LVL = 2
N_SUB = 2


def draw_mask_words(key, part):
    key = jax.random.fold_in(key, 11)
    words = jax.random.randint(key, (NODES, 8), 0, 65536, dtype=jnp.int32)
    return words.at[0, 0].set(65535)


def distinct_order(key, count):
    scores = jax.random.randint(key, (count,), 0, 1 << 20, dtype=jnp.int32)
    scores = scores * count + jnp.arange(count, dtype=jnp.int32)
    return jnp.argsort(scores).astype(jnp.int32)


def draw_partner(key, part):
    key = jax.random.fold_in(key, 12)
    key_order = jax.random.fold_in(key, 1)
    key_masks = jax.random.fold_in(key, 2)
    key_round = jax.random.fold_in(key, 3)
    key_split = jax.random.fold_in(key, 4)
    order = distinct_order(key_order, N_DOM)
    masks = distinct_order(key_masks, N_DOM - 1) + 1
    single_round = jax.random.randint(key_round, (), 0, ROUNDS, dtype=jnp.int32)
    split_bits = jax.random.randint(key_split, (N_DOM,), 0, 2, dtype=jnp.int32)
    places = jnp.arange(N_DOM, dtype=jnp.int32)
    round_rows = []
    for round_number in range(ROUNDS):
        paired = jnp.bitwise_xor(places, masks[round_number])
        split_here = jnp.logical_and(single_round == round_number, split_bits[jnp.minimum(places, paired)] == 1)
        target = jnp.where(split_here, places, paired)
        round_rows.append(jnp.zeros((N_DOM,), jnp.int32).at[order].set(order[target]))
    return jnp.stack(round_rows)


def draw_live_counts(key, part):
    key = jax.random.fold_in(key, 13)
    key_counts, key_spot = jax.random.split(key)
    counts = jax.random.randint(key_counts, (PIECES,), NODE_DEV // 4, NODE_DEV + 1, dtype=jnp.int32)
    full_piece = jax.random.randint(key_spot, (), 0, PIECES, dtype=jnp.int32)
    return counts.at[full_piece].set(NODE_DEV)


def set_ends(values, own_key, least, high):
    index_at = [jax.random.randint(jax.random.fold_in(own_key, axis), (), 0, length) for axis, length in enumerate(values.shape)]
    widest = values.shape.index(max(values.shape))
    beside = index_at[:widest] + [(index_at[widest] + 1) % values.shape[widest]] + index_at[widest + 1:]
    return values.at[tuple(index_at)].set(least).at[tuple(beside)].set(high)


def shard_levels(stream_key, shape, shards, least, high):
    def one(position, parts):
        heights = jax.random.uniform(jax.random.fold_in(jax.random.fold_in(stream_key, 6), position), (parts,), jnp.float32, least / len(shards), high / len(shards))
        return jnp.repeat(jnp.exp(heights), shape[position] // parts).reshape((-1,) + (1,) * (len(shape) - position - 1))

    level = one(*shards[0])
    for cut in shards[1:]:
        level = level * one(*cut)
    return level


def bell_draw(own_key, extent, deviation, most, cuts=(), kind=jnp.bfloat16):
    factor_of = shard_levels(own_key, extent, cuts, -0.22, 0.18) if cuts else 1.0
    entries = jax.random.normal(own_key, extent, jnp.float32) * deviation * factor_of
    return jnp.minimum(jnp.maximum(entries, -most), most).astype(kind)


def setup_inputs(seed: int = 0, part: int = 0) -> dict:
    key_of = jax.random.split(jax.random.key(seed), 12)
    part_keys = jax.random.split(jax.random.fold_in(key_of[11], part), 12)
    node_latents = bell_draw(part_keys[0], (NODES, H), 1.0, 6.0, ((0, 16),))
    coarse_latents = bell_draw(part_keys[1], (COARSE, H), 1.0, 6.0, ((0, 16),))
    cotangent = bell_draw(part_keys[2], (NODES, H), 1.0, 6.0, ((0, 16),))
    w_message = bell_draw(key_of[3], (H, H), H ** -0.5, 0.25)
    w_coarse = bell_draw(key_of[4], (H, H), H ** -0.5, 0.25)
    w_update = bell_draw(key_of[5], (H, H), H ** -0.5, 0.25)
    mask_words = draw_mask_words(jax.random.fold_in(jax.random.fold_in(key_of[11], part), 71), part)
    tile_index = set_ends(jax.random.randint(part_keys[7], (PIECES * ROUNDS, BT), 0, NODE_DEV), jax.random.fold_in(part_keys[7], 1), 0, NODE_DEV - 1).astype(jnp.int32)
    partner = draw_partner(jax.random.fold_in(jax.random.fold_in(key_of[11], part), 71), part)
    assignment = set_ends(jax.random.randint(part_keys[9], (NODES,), 0, GROUP_ROWS), jax.random.fold_in(part_keys[9], 1), 0, GROUP_ROWS - 1).astype(jnp.int32)
    live_counts = draw_live_counts(jax.random.fold_in(jax.random.fold_in(key_of[11], part), 71), part)
    return dict(node_latents=node_latents, coarse_latents=coarse_latents, cotangent=cotangent, w_message=w_message, w_coarse=w_coarse, w_update=w_update, mask_words=mask_words, tile_index=tile_index, partner=partner, assignment=assignment, live_counts=live_counts)


def silu_slope(values):
    logistic = jax.nn.sigmoid(values)
    return logistic * (1.0 + values * (1.0 - logistic))


def unpack_mask(words):
    columns = np.arange(128)
    picked = jnp.take(words, jnp.asarray(columns // 16, dtype=jnp.int32), axis=1)
    shifts = jnp.asarray(columns % 16, dtype=jnp.int32)
    return jnp.bitwise_and(jnp.right_shift(picked, shifts[None, :]), 1)


def reference(node_latents, coarse_latents, cotangent, w_message, w_coarse, w_update, mask_words, tile_index, partner, assignment, live_counts):
    hidden = node_latents.shape[1]
    pieces = N_DOM * N_LVL * N_SUB
    piece_ids = jnp.arange(pieces, dtype=jnp.int32)
    dom_of = piece_ids // (N_LVL * N_SUB)
    rest_of = piece_ids % (N_LVL * N_SUB)
    sub_of = rest_of % N_SUB
    live = (jnp.arange(NODE_DEV, dtype=jnp.int32)[None, :] < live_counts[:, None]).reshape(NODES, 1)
    pre_msg = jnp.dot(node_latents, w_message, preferred_element_type=jnp.float32)
    message = jnp.where(live, jax.nn.silu(pre_msg), 0.0).astype(jnp.bfloat16)
    pre_crs = jnp.dot(coarse_latents, w_coarse, preferred_element_type=jnp.float32)
    coarse_msg = jax.nn.silu(pre_crs).astype(jnp.bfloat16)
    adjacency = unpack_mask(mask_words).astype(jnp.float32).reshape(NODES // 128, 128, 128)

    def local_sum(values, form):
        blocks = values.astype(jnp.float32).reshape(NODES // 128, 128, hidden)
        return jnp.einsum(form, adjacency, blocks).reshape(NODES, hidden)

    tile_rows = tile_index.reshape(pieces, ROUNDS, BT) + (piece_ids * NODE_DEV)[:, None, None]
    peer_piece = jnp.transpose(partner)[dom_of] * (N_LVL * N_SUB) + rest_of[:, None]
    peer_rows = tile_rows[peer_piece, jnp.arange(ROUNDS, dtype=jnp.int32)[None, :]]
    own_flat = tile_rows.reshape(-1)
    peer_flat = peer_rows.reshape(-1)

    def boundary(values):
        return jnp.zeros((NODES, hidden), jnp.float32).at[own_flat].add(values[peer_flat].astype(jnp.float32))

    assign = assignment.reshape(pieces, NODE_DEV)
    coarse_row = ((dom_of[:, None] * N_LVL + assign // CD) * N_SUB + sub_of[:, None]) * CD + assign % CD
    coarse_row = coarse_row.reshape(NODES)

    aggregate = 0.125 * local_sum(message, "bij,bjh->bih") + boundary(message) + coarse_msg[coarse_row].astype(jnp.float32)
    aggregate = aggregate.astype(jnp.bfloat16)
    pre_upd = jnp.dot(aggregate, w_update, preferred_element_type=jnp.float32)
    updated = (node_latents.astype(jnp.float32) + jnp.where(live, jax.nn.silu(pre_upd), 0.0)).astype(jnp.bfloat16)

    d_pre_upd = jnp.where(live, cotangent.astype(jnp.float32) * silu_slope(pre_upd), 0.0).astype(jnp.bfloat16)
    d_agg = jnp.dot(d_pre_upd, jnp.transpose(w_update), preferred_element_type=jnp.float32).astype(jnp.bfloat16)
    d_message = 0.125 * local_sum(d_agg, "bji,bjh->bih") + boundary(d_agg)
    d_pre_msg = jnp.where(live, d_message * silu_slope(pre_msg), 0.0).astype(jnp.bfloat16)
    d_nodes = (cotangent.astype(jnp.float32) + jnp.dot(d_pre_msg, jnp.transpose(w_message), preferred_element_type=jnp.float32)).astype(jnp.bfloat16)
    d_coarse_msg = jnp.zeros((COARSE, hidden), jnp.float32).at[coarse_row].add(d_agg.astype(jnp.float32))
    d_pre_crs = (d_coarse_msg * silu_slope(pre_crs)).astype(jnp.bfloat16)
    d_coarse = jnp.dot(d_pre_crs, jnp.transpose(w_coarse), preferred_element_type=jnp.float32).astype(jnp.bfloat16)
    return updated, d_nodes, d_coarse
```

```python
import functools

import jax
import jax.numpy as jnp
from jax import lax
from jax.experimental import pallas as pl
from jax.experimental.pallas import tpu as pltpu
from jax.sharding import PartitionSpec as P

BLOCK = 128
MESH = pl.DeviceIdType.MESH


def gate(values):
    return 0.5 * jnp.tanh(0.5 * values) + 0.5


def dot(left, right, left_dim=1, right_dim=0):
    return lax.dot_general(
        left, right, (((left_dim,), (right_dim,)), ((), ())), preferred_element_type=jnp.float32
    )


def layer_kernel(
    n_dom,
    n_lvl,
    node_hbm,
    coarse_hbm,
    cot_hbm,
    w_message_hbm,
    w_coarse_hbm,
    w_update_hbm,
    words_hbm,
    tile_hbm,
    partner_hbm,
    assign_hbm,
    live_hbm,
    updated_hbm,
    d_nodes_hbm,
    d_coarse_hbm,
    node,
    coarse,
    cot,
    w_message,
    w_coarse,
    w_update,
    words,
    tile,
    partner,
    assign,
    live,
    adj_back,
    adj_fore,
    spread,
    gather,
    picker,
    pick_back,
    message,
    slope_msg,
    slope_crs,
    aggregate,
    d_agg,
    d_pre,
    updated,
    d_nodes,
    d_coarse,
    send_one,
    land_one,
    send_two,
    land_two,
    coarse_all,
    d_own,
    d_land,
    in_sem,
    out_sem,
    send_sem,
    one_sem,
    two_sem,
    crs_send_sem,
    crs_sem,
    grad_send_sem,
    grad_sem,
):
    rows, hidden = node.shape
    blocks = rows // BLOCK
    c_rows = coarse.shape[0]
    rounds, width = tile.shape
    tiles = n_dom * width
    me = lax.axis_index("dom")
    level = lax.axis_index("lvl")
    doms = [lax.rem(me + step, n_dom) for step in range(1, n_dom)]
    lvls = [lax.rem(level + step, n_lvl) for step in range(1, n_lvl)]

    barrier = pltpu.get_barrier_semaphore()
    for other in doms:
        pl.semaphore_signal(barrier, inc=1, device_id={"dom": other}, device_id_type=MESH)
    for other in lvls:
        pl.semaphore_signal(barrier, inc=1, device_id={"lvl": other}, device_id_type=MESH)

    pairs = dict(
        tile=(tile_hbm, tile),
        partner=(partner_hbm, partner),
        live=(live_hbm, live),
        node=(node_hbm, node),
        w_message=(w_message_hbm, w_message),
        coarse=(coarse_hbm, coarse),
        w_coarse=(w_coarse_hbm, w_coarse),
        words=(words_hbm, words),
        assign=(assign_hbm, assign),
        cot=(cot_hbm, cot),
        w_update=(w_update_hbm, w_update),
    )
    loads = {
        name: pltpu.make_async_copy(pair[0], pair[1], in_sem.at[i])
        for i, (name, pair) in enumerate(pairs.items())
    }
    for load in loads.values():
        load.start()

    def trade(source, landing, landing_sem, base):
        own = pl.ds(pl.multiple_of(me * width, width), width)
        copies = []
        for i, other in enumerate(doms):
            copy = pltpu.make_async_remote_copy(
                src_ref=source.at[pl.ds(pl.multiple_of(other * width, width), width)],
                dst_ref=landing.at[own],
                send_sem=send_sem.at[base + i],
                recv_sem=landing_sem.at[i],
                device_id={"dom": other},
                device_id_type=MESH,
            )
            copy.start()
            copies.append(copy)
        landing[own, :] = source[own, :]
        return copies

    loads["tile"].wait()
    loads["partner"].wait()
    loads["live"].wait()
    count = live[0]
    peer_of = lax.broadcasted_iota(jnp.int32, (1, tiles), 1) // width
    target = jnp.full((1, tiles), -1, jnp.int32)
    for r in range(rounds):
        wide = jnp.concatenate([tile[r : r + 1, :]] * n_dom, axis=1)
        target = jnp.where(peer_of == partner[r, me], wide, target)
    place = lax.broadcasted_iota(jnp.int32, (rows, tiles), 0)
    spread_f = jnp.where(place == target, 1.0, 0.0)
    spread[...] = spread_f.astype(jnp.bfloat16)
    gather_f = jnp.transpose(spread_f)
    gather[...] = gather_f.astype(jnp.bfloat16)
    lane = lax.broadcasted_iota(jnp.int32, (tiles, rows), 1)
    live_t = jnp.sum(jnp.where(lane < count, gather_f, 0.0), axis=1, keepdims=True)

    loads["node"].wait()
    loads["w_message"].wait()
    node_t = dot(gather[...], node[...]).astype(jnp.bfloat16)
    pre_t = dot(node_t, w_message[...])
    send_one[...] = (live_t * (pre_t * gate(pre_t))).astype(jnp.bfloat16)
    pl.semaphore_wait(barrier, n_dom - 1 + n_lvl - 1)
    sent = trade(send_one, land_one, one_sem, 0)

    loads["coarse"].wait()
    loads["w_coarse"].wait()
    pre_crs = dot(coarse[...], w_coarse[...])
    gate_crs = gate(pre_crs)
    silu_crs = pre_crs * gate_crs
    slope_crs[...] = gate_crs + silu_crs * (1.0 - gate_crs)
    own_crs = pl.ds(pl.multiple_of(level * c_rows, c_rows), c_rows)
    coarse_all[own_crs, :] = silu_crs.astype(jnp.bfloat16)
    crs_copies = []
    for i, other in enumerate(lvls):
        copy = pltpu.make_async_remote_copy(
            src_ref=coarse_all.at[own_crs],
            dst_ref=coarse_all.at[own_crs],
            send_sem=crs_send_sem.at[i],
            recv_sem=crs_sem.at[i],
            device_id={"lvl": other},
            device_id_type=MESH,
        )
        copy.start()
        crs_copies.append(copy)

    def live_rows(block):
        at = lax.broadcasted_iota(jnp.int32, (BLOCK, hidden), 0) + block * BLOCK
        return at < count

    for b in range(blocks):
        part = pl.ds(b * BLOCK, BLOCK)
        pre = dot(node[part, :], w_message[...])
        g = gate(pre)
        silu = pre * g
        alive = live_rows(b)
        message[part, :] = jnp.where(alive, silu, 0.0).astype(jnp.bfloat16)
        slope_msg[part, :] = jnp.where(alive, g + silu * (1.0 - g), 0.0)

    loads["words"].wait()
    loads["assign"].wait()
    bits = jnp.concatenate(
        [jnp.broadcast_to(words[w : w + 1, :], (16, rows)) for w in range(BLOCK // 16)], axis=0
    )
    shift = lax.broadcasted_iota(jnp.int32, (BLOCK, rows), 0) % 16
    bits = jnp.bitwise_and(jnp.right_shift(bits, shift), 1)
    adj_f = 0.125 * bits.astype(jnp.float32)
    adj_back[...] = adj_f.astype(jnp.bfloat16)
    adj_fore[...] = jnp.transpose(adj_f).astype(jnp.bfloat16)
    coarse_at = lax.broadcasted_iota(jnp.int32, (n_lvl * c_rows, rows), 0)
    pick_f = jnp.where(coarse_at == assign[...], 1.0, 0.0)
    pick_back[...] = pick_f.astype(jnp.bfloat16)
    picker[...] = jnp.transpose(pick_f).astype(jnp.bfloat16)
    loads["cot"].wait()
    cot_t = dot(gather[...], cot[...])

    for copy in sent:
        copy.wait_recv()
    for copy in crs_copies:
        copy.wait_recv()

    for b in range(blocks):
        part = pl.ds(b * BLOCK, BLOCK)
        total = dot(adj_fore[part, :], message[part, :])
        total += dot(spread[part, :], land_one[...])
        total += dot(picker[part, :], coarse_all[...])
        aggregate[part, :] = total.astype(jnp.bfloat16)

    loads["w_update"].wait()
    agg_t = dot(gather[...], aggregate[...]).astype(jnp.bfloat16)
    pre_t = dot(agg_t, w_update[...])
    g = gate(pre_t)
    d_t = (live_t * cot_t * (g * (1.0 + pre_t * (1.0 - g)))).astype(jnp.bfloat16)
    send_two[...] = dot(d_t, w_update[...], 1, 1).astype(jnp.bfloat16)
    sent_two = trade(send_two, land_two, two_sem, n_dom - 1)

    for b in range(blocks):
        part = pl.ds(b * BLOCK, BLOCK)
        pre = dot(aggregate[part, :], w_update[...])
        g = gate(pre)
        silu = pre * g
        alive = live_rows(b)
        slope = g + silu * (1.0 - g)
        updated[part, :] = (
            node[part, :].astype(jnp.float32) + jnp.where(alive, silu, 0.0)
        ).astype(jnp.bfloat16)
        d_pre[part, :] = jnp.where(alive, cot[part, :].astype(jnp.float32) * slope, 0.0).astype(
            jnp.bfloat16
        )
        d_agg[part, :] = dot(d_pre[part, :], w_update[...], 1, 1).astype(jnp.bfloat16)
    stores = [pltpu.make_async_copy(updated, updated_hbm, out_sem.at[0])]
    stores[0].start()

    d_own[...] = dot(pick_back[...], d_agg[...])
    grad_copies = []
    for i, other in enumerate(lvls):
        copy = pltpu.make_async_remote_copy(
            src_ref=d_own.at[pl.ds(pl.multiple_of(other * c_rows, c_rows), c_rows)],
            dst_ref=d_land.at[i],
            send_sem=grad_send_sem.at[i],
            recv_sem=grad_sem.at[i],
            device_id={"lvl": other},
            device_id_type=MESH,
        )
        copy.start()
        grad_copies.append(copy)

    for copy in sent_two:
        copy.wait_recv()
    for b in range(blocks):
        part = pl.ds(b * BLOCK, BLOCK)
        total = dot(adj_back[:, part], d_agg[part, :])
        total += dot(spread[part, :], land_two[...])
        d_pre_msg = (total * slope_msg[part, :]).astype(jnp.bfloat16)
        d_nodes[part, :] = (
            cot[part, :].astype(jnp.float32) + dot(d_pre_msg, w_message[...], 1, 1)
        ).astype(jnp.bfloat16)
    stores.append(pltpu.make_async_copy(d_nodes, d_nodes_hbm, out_sem.at[1]))
    stores[1].start()

    total = d_own[own_crs, :]
    for i, copy in enumerate(grad_copies):
        copy.wait_recv()
        total += d_land[i]
    d_pre_crs = (total * slope_crs[...]).astype(jnp.bfloat16)
    d_coarse[...] = dot(d_pre_crs, w_coarse[...], 1, 1).astype(jnp.bfloat16)
    stores.append(pltpu.make_async_copy(d_coarse, d_coarse_hbm, out_sem.at[2]))
    stores[2].start()

    for copy in sent + crs_copies + sent_two + grad_copies:
        copy.wait_send()
    for store in stores:
        store.wait()


def on_device(
    n_dom,
    n_lvl,
    node_latents,
    coarse_latents,
    cotangent,
    w_message,
    w_coarse,
    w_update,
    mask_words,
    tile_index,
    partner,
    assignment,
    live_counts,
):
    rows, hidden = node_latents.shape
    c_rows = coarse_latents.shape[0]
    rounds, width = tile_index.shape
    tiles = n_dom * width
    group = n_lvl * c_rows
    bf16, f32, i32 = jnp.bfloat16, jnp.float32, jnp.int32
    vmem = pltpu.VMEM
    dma = pltpu.SemaphoreType.DMA
    scratch = [
        vmem((rows, hidden), bf16),
        vmem((c_rows, hidden), bf16),
        vmem((rows, hidden), bf16),
        vmem((hidden, hidden), bf16),
        vmem((hidden, hidden), bf16),
        vmem((hidden, hidden), bf16),
        vmem((8, rows), i32),
        vmem((rounds, width), i32),
        pltpu.SMEM((rounds, n_dom), i32),
        vmem((1, rows), i32),
        pltpu.SMEM((1,), i32),
        vmem((BLOCK, rows), bf16),
        vmem((rows, BLOCK), bf16),
        vmem((rows, tiles), bf16),
        vmem((tiles, rows), bf16),
        vmem((rows, group), bf16),
        vmem((group, rows), bf16),
        vmem((rows, hidden), bf16),
        vmem((rows, hidden), f32),
        vmem((c_rows, hidden), f32),
        vmem((rows, hidden), bf16),
        vmem((rows, hidden), bf16),
        vmem((rows, hidden), bf16),
        vmem((rows, hidden), bf16),
        vmem((rows, hidden), bf16),
        vmem((c_rows, hidden), bf16),
        vmem((tiles, hidden), bf16),
        vmem((tiles, hidden), bf16),
        vmem((tiles, hidden), bf16),
        vmem((tiles, hidden), bf16),
        vmem((group, hidden), bf16),
        vmem((group, hidden), f32),
        vmem((n_lvl - 1, c_rows, hidden), f32),
        dma((11,)),
        dma((3,)),
        dma((2 * (n_dom - 1),)),
        dma((n_dom - 1,)),
        dma((n_dom - 1,)),
        dma((n_lvl - 1,)),
        dma((n_lvl - 1,)),
        dma((n_lvl - 1,)),
        dma((n_lvl - 1,)),
    ]
    anywhere = pl.BlockSpec(memory_space=pl.ANY)
    return pl.pallas_call(
        functools.partial(layer_kernel, n_dom, n_lvl),
        out_shape=(
            jax.ShapeDtypeStruct((rows, hidden), bf16),
            jax.ShapeDtypeStruct((rows, hidden), bf16),
            jax.ShapeDtypeStruct((c_rows, hidden), bf16),
        ),
        in_specs=[anywhere] * 11,
        out_specs=(anywhere,) * 3,
        scratch_shapes=scratch,
        compiler_params=pltpu.CompilerParams(
            collective_id=0, has_side_effects=True, vmem_limit_bytes=48 * 1024 * 1024
        ),
        name="layer",
    )(
        node_latents,
        coarse_latents,
        cotangent,
        w_message,
        w_coarse,
        w_update,
        jnp.transpose(mask_words),
        tile_index,
        partner,
        assignment.reshape(1, rows),
        live_counts,
    )


def solution(mesh):
    pieces = P(("grp", "dom", "lvl", "sub"), None)
    flat = P(("grp", "dom", "lvl", "sub"))
    return jax.shard_map(
        functools.partial(on_device, mesh.shape["dom"], mesh.shape["lvl"]),
        mesh=mesh,
        in_specs=(
            pieces,
            pieces,
            pieces,
            P(),
            P(),
            P(),
            pieces,
            pieces,
            P("grp", None),
            flat,
            flat,
        ),
        out_specs=(pieces, pieces, pieces),
        check_vma=False,
    )
```

```python
import functools

import jax
import jax.numpy as jnp
from jax import lax
from jax.experimental import pallas as pl
from jax.experimental.pallas import tpu as pltpu
from jax.sharding import PartitionSpec as P

BLOCK = 128
MESH = pl.DeviceIdType.MESH


def gate(values):
    return 0.5 * jnp.tanh(0.5 * values) + 0.5


def dot(left, right, left_dim=1, right_dim=0):
    return lax.dot_general(
        left, right, (((left_dim,), (right_dim,)), ((), ())), preferred_element_type=jnp.float32
    )


def layer_kernel(
    n_dom,
    n_lvl,
    node_hbm,
    coarse_hbm,
    cot_hbm,
    w_message_hbm,
    w_coarse_hbm,
    w_update_hbm,
    words_hbm,
    tile_hbm,
    partner_hbm,
    assign_hbm,
    live_hbm,
    updated_hbm,
    d_nodes_hbm,
    d_coarse_hbm,
    node,
    coarse,
    cot,
    w_message,
    w_coarse,
    w_update,
    words,
    tile,
    partner,
    assign,
    live,
    adj_back,
    adj_fore,
    spread,
    gather,
    picker,
    pick_back,
    message,
    slope_msg,
    slope_crs,
    aggregate,
    d_agg,
    d_pre,
    updated,
    d_nodes,
    d_coarse,
    send_one,
    land_one,
    send_two,
    land_two,
    coarse_all,
    d_own,
    d_land,
    in_sem,
    out_sem,
    send_sem,
    one_sem,
    two_sem,
    crs_send_sem,
    crs_sem,
    grad_send_sem,
    grad_sem,
):
    rows, hidden = node.shape
    blocks = rows // BLOCK
    c_rows = coarse.shape[0]
    rounds, width = tile.shape
    tiles = n_dom * width
    me = lax.axis_index("dom")
    level = lax.axis_index("lvl")
    doms = [lax.rem(me + step, n_dom) for step in range(1, n_dom)]
    lvls = [lax.rem(level + step, n_lvl) for step in range(1, n_lvl)]

    barrier = pltpu.get_barrier_semaphore()
    for other in doms:
        pl.semaphore_signal(barrier, inc=1, device_id={"dom": other}, device_id_type=MESH)
    for other in lvls:
        pl.semaphore_signal(barrier, inc=1, device_id={"lvl": other}, device_id_type=MESH)

    pairs = dict(
        tile=(tile_hbm, tile),
        partner=(partner_hbm, partner),
        live=(live_hbm, live),
        node=(node_hbm, node),
        w_message=(w_message_hbm, w_message),
        coarse=(coarse_hbm, coarse),
        w_coarse=(w_coarse_hbm, w_coarse),
        words=(words_hbm, words),
        assign=(assign_hbm, assign),
        cot=(cot_hbm, cot),
        w_update=(w_update_hbm, w_update),
    )
    loads = {
        name: pltpu.make_async_copy(pair[0], pair[1], in_sem.at[i])
        for i, (name, pair) in enumerate(pairs.items())
    }
    for load in loads.values():
        load.start()

    def trade(source, landing, landing_sem, base):
        own = pl.ds(pl.multiple_of(me * width, width), width)
        copies = []
        for i, other in enumerate(doms):
            copy = pltpu.make_async_remote_copy(
                src_ref=source.at[pl.ds(pl.multiple_of(other * width, width), width)],
                dst_ref=landing.at[own],
                send_sem=send_sem.at[base + i],
                recv_sem=landing_sem.at[i],
                device_id={"dom": other},
                device_id_type=MESH,
            )
            copy.start()
            copies.append(copy)
        landing[own, :] = source[own, :]
        return copies

    loads["tile"].wait()
    loads["partner"].wait()
    loads["live"].wait()
    count = live[0]
    peer_of = lax.broadcasted_iota(jnp.int32, (1, tiles), 1) // width
    target = jnp.full((1, tiles), -1, jnp.int32)
    for r in range(rounds):
        wide = jnp.concatenate([tile[r : r + 1, :]] * n_dom, axis=1)
        target = jnp.where(peer_of == partner[r, me], wide, target)
    place = lax.broadcasted_iota(jnp.int32, (rows, tiles), 0)
    spread_f = jnp.where(place == target, 1.0, 0.0)
    spread[...] = spread_f.astype(jnp.bfloat16)
    gather_f = jnp.transpose(spread_f)
    gather[...] = gather_f.astype(jnp.bfloat16)
    lane = lax.broadcasted_iota(jnp.int32, (tiles, rows), 1)
    live_t = jnp.sum(jnp.where(lane < count, gather_f, 0.0), axis=1, keepdims=True)

    loads["node"].wait()
    loads["w_message"].wait()
    node_t = dot(gather[...], node[...]).astype(jnp.bfloat16)
    pre_t = dot(node_t, w_message[...])
    send_one[...] = (live_t * (pre_t * gate(pre_t))).astype(jnp.bfloat16)
    pl.semaphore_wait(barrier, n_dom - 1 + n_lvl - 1)
    sent = trade(send_one, land_one, one_sem, 0)

    loads["coarse"].wait()
    loads["w_coarse"].wait()
    pre_crs = dot(coarse[...], w_coarse[...])
    gate_crs = gate(pre_crs)
    silu_crs = pre_crs * gate_crs
    slope_crs[...] = gate_crs + silu_crs * (1.0 - gate_crs)
    own_crs = pl.ds(pl.multiple_of(level * c_rows, c_rows), c_rows)
    coarse_all[own_crs, :] = silu_crs.astype(jnp.bfloat16)
    crs_copies = []
    for i, other in enumerate(lvls):
        copy = pltpu.make_async_remote_copy(
            src_ref=coarse_all.at[own_crs],
            dst_ref=coarse_all.at[own_crs],
            send_sem=crs_send_sem.at[i],
            recv_sem=crs_sem.at[i],
            device_id={"lvl": other},
            device_id_type=MESH,
        )
        copy.start()
        crs_copies.append(copy)

    def live_rows(block):
        at = lax.broadcasted_iota(jnp.int32, (BLOCK, hidden), 0) + block * BLOCK
        return at < count

    for b in range(blocks):
        part = pl.ds(b * BLOCK, BLOCK)
        pre = dot(node[part, :], w_message[...])
        g = gate(pre)
        silu = pre * g
        alive = live_rows(b)
        message[part, :] = jnp.where(alive, silu, 0.0).astype(jnp.bfloat16)
        slope_msg[part, :] = jnp.where(alive, g + silu * (1.0 - g), 0.0)

    loads["words"].wait()
    loads["assign"].wait()
    bits = jnp.concatenate(
        [jnp.broadcast_to(words[w : w + 1, :], (16, rows)) for w in range(BLOCK // 16)], axis=0
    )
    shift = lax.broadcasted_iota(jnp.int32, (BLOCK, rows), 0) % 16
    bits = jnp.bitwise_and(jnp.right_shift(bits, shift), 1)
    adj_f = 0.125 * bits.astype(jnp.float32)
    adj_back[...] = adj_f.astype(jnp.bfloat16)
    adj_fore[...] = jnp.transpose(adj_f).astype(jnp.bfloat16)
    coarse_at = lax.broadcasted_iota(jnp.int32, (n_lvl * c_rows, rows), 0)
    pick_f = jnp.where(coarse_at == assign[...].reshape(1, rows), 1.0, 0.0)
    pick_back[...] = pick_f.astype(jnp.bfloat16)
    picker[...] = jnp.transpose(pick_f).astype(jnp.bfloat16)
    loads["cot"].wait()
    cot_t = dot(gather[...], cot[...])

    for copy in sent:
        copy.wait_recv()
    for copy in crs_copies:
        copy.wait_recv()

    for b in range(blocks):
        part = pl.ds(b * BLOCK, BLOCK)
        total = dot(adj_fore[part, :], message[part, :])
        total += dot(spread[part, :], land_one[...])
        total += dot(picker[part, :], coarse_all[...])
        aggregate[part, :] = total.astype(jnp.bfloat16)

    loads["w_update"].wait()
    agg_t = dot(gather[...], aggregate[...]).astype(jnp.bfloat16)
    pre_t = dot(agg_t, w_update[...])
    g = gate(pre_t)
    d_t = (live_t * cot_t * (g * (1.0 + pre_t * (1.0 - g)))).astype(jnp.bfloat16)
    send_two[...] = dot(d_t, w_update[...], 1, 1).astype(jnp.bfloat16)
    sent_two = trade(send_two, land_two, two_sem, n_dom - 1)

    for b in range(blocks):
        part = pl.ds(b * BLOCK, BLOCK)
        pre = dot(aggregate[part, :], w_update[...])
        g = gate(pre)
        silu = pre * g
        alive = live_rows(b)
        slope = g + silu * (1.0 - g)
        updated[part, :] = (
            node[part, :].astype(jnp.float32) + jnp.where(alive, silu, 0.0)
        ).astype(jnp.bfloat16)
        d_pre[part, :] = jnp.where(alive, cot[part, :].astype(jnp.float32) * slope, 0.0).astype(
            jnp.bfloat16
        )
        d_agg[part, :] = dot(d_pre[part, :], w_update[...], 1, 1).astype(jnp.bfloat16)

    stores = [pltpu.make_async_copy(updated, updated_hbm, out_sem.at[0])]
    stores[0].start()

    d_own[...] = dot(pick_back[...], d_agg[...])
    grad_copies = []
    for i, other in enumerate(lvls):
        copy = pltpu.make_async_remote_copy(
            src_ref=d_own.at[pl.ds(pl.multiple_of(other * c_rows, c_rows), c_rows)],
            dst_ref=d_land.at[i],
            send_sem=grad_send_sem.at[i],
            recv_sem=grad_sem.at[i],
            device_id={"lvl": other},
            device_id_type=MESH,
        )
        copy.start()
        grad_copies.append(copy)

    for copy in sent_two:
        copy.wait_recv()
    for b in range(blocks):
        part = pl.ds(b * BLOCK, BLOCK)
        total = dot(adj_back[:, part], d_agg[part, :])
        total += dot(spread[part, :], land_two[...])
        d_pre_msg = (total * slope_msg[part, :]).astype(jnp.bfloat16)
        d_nodes[part, :] = (
            cot[part, :].astype(jnp.float32) + dot(d_pre_msg, w_message[...], 1, 1)
        ).astype(jnp.bfloat16)

    stores.append(pltpu.make_async_copy(d_nodes, d_nodes_hbm, out_sem.at[1]))
    stores[1].start()

    total = d_own[own_crs, :]
    for i, copy in enumerate(grad_copies):
        copy.wait_recv()
        total += d_land[i]
    d_pre_crs = (total * slope_crs[...]).astype(jnp.bfloat16)
    d_coarse[...] = dot(d_pre_crs, w_coarse[...], 1, 1).astype(jnp.bfloat16)

    stores.append(pltpu.make_async_copy(d_coarse, d_coarse_hbm, out_sem.at[2]))
    stores[2].start()
    for copy in sent + crs_copies + sent_two + grad_copies:
        copy.wait_send()
    for store in stores:
        store.wait()


def store_kernel(updated, d_nodes, d_coarse, *refs):
    outs, stages, in_sem, out_sem = refs[:3], refs[3:6], refs[6], refs[7]
    parts = []
    for i, ref in enumerate((updated, d_nodes, d_coarse)):
        rows = ref.shape[0]
        step = min(rows, 256)
        parts += [(i, pl.ds(start, step)) for start in range(0, rows, step)]
    sources = (updated, d_nodes, d_coarse)
    loads = [
        pltpu.make_async_copy(sources[i].at[at], stages[i].at[at], in_sem.at[n])
        for n, (i, at) in enumerate(parts)
    ]
    stores = [
        pltpu.make_async_copy(stages[i].at[at], outs[i].at[at], out_sem.at[n])
        for n, (i, at) in enumerate(parts)
    ]
    for load in loads:
        load.start()
    for load, store in zip(loads, stores):
        load.wait()
        store.start()
    for store in stores:
        store.wait()


def on_device(
    n_dom,
    n_lvl,
    node_latents,
    coarse_latents,
    cotangent,
    w_message,
    w_coarse,
    w_update,
    mask_words,
    tile_index,
    partner,
    assignment,
    live_counts,
):
    rows, hidden = node_latents.shape
    c_rows = coarse_latents.shape[0]
    rounds, width = tile_index.shape
    tiles = n_dom * width
    group = n_lvl * c_rows
    bf16, f32, i32 = jnp.bfloat16, jnp.float32, jnp.int32
    vmem = pltpu.VMEM
    dma = pltpu.SemaphoreType.DMA
    scratch = [
        vmem((rows, hidden), bf16),
        vmem((c_rows, hidden), bf16),
        vmem((rows, hidden), bf16),
        vmem((hidden, hidden), bf16),
        vmem((hidden, hidden), bf16),
        vmem((hidden, hidden), bf16),
        vmem((8, rows), i32),
        vmem((rounds, width), i32),
        pltpu.SMEM((rounds, n_dom), i32),
        vmem((rows,), i32),
        pltpu.SMEM((1,), i32),
        vmem((BLOCK, rows), bf16),
        vmem((rows, BLOCK), bf16),
        vmem((rows, tiles), bf16),
        vmem((tiles, rows), bf16),
        vmem((rows, group), bf16),
        vmem((group, rows), bf16),
        vmem((rows, hidden), bf16),
        vmem((rows, hidden), f32),
        vmem((c_rows, hidden), f32),
        vmem((rows, hidden), bf16),
        vmem((rows, hidden), bf16),
        vmem((rows, hidden), bf16),
        vmem((rows, hidden), bf16),
        vmem((rows, hidden), bf16),
        vmem((c_rows, hidden), bf16),
        vmem((tiles, hidden), bf16),
        vmem((tiles, hidden), bf16),
        vmem((tiles, hidden), bf16),
        vmem((tiles, hidden), bf16),
        vmem((group, hidden), bf16),
        vmem((group, hidden), f32),
        vmem((n_lvl - 1, c_rows, hidden), f32),
        dma((11,)),
        dma((3,)),
        dma((2 * (n_dom - 1),)),
        dma((n_dom - 1,)),
        dma((n_dom - 1,)),
        dma((n_lvl - 1,)),
        dma((n_lvl - 1,)),
        dma((n_lvl - 1,)),
        dma((n_lvl - 1,)),
    ]
    far = pl.BlockSpec(memory_space=pl.ANY)
    outs = (
        jax.ShapeDtypeStruct((rows, hidden), bf16),
        jax.ShapeDtypeStruct((rows, hidden), bf16),
        jax.ShapeDtypeStruct((c_rows, hidden), bf16),
    )
    results = pl.pallas_call(
        functools.partial(layer_kernel, n_dom, n_lvl),
        out_shape=outs,
        in_specs=[far] * 11,
        out_specs=(far,) * 3,
        scratch_shapes=scratch,
        compiler_params=pltpu.CompilerParams(
            collective_id=0, has_side_effects=True, vmem_limit_bytes=56 * 1024 * 1024
        ),
        name="layer",
    )(
        node_latents,
        coarse_latents,
        cotangent,
        w_message,
        w_coarse,
        w_update,
        jnp.transpose(mask_words),
        tile_index,
        partner,
        assignment,
        live_counts,
    )
    return pl.pallas_call(
        store_kernel,
        out_shape=outs,
        in_specs=[far] * 3,
        out_specs=(far,) * 3,
        scratch_shapes=[vmem(out.shape, bf16) for out in outs] + [dma((7,)), dma((7,))],
        compiler_params=pltpu.CompilerParams(vmem_limit_bytes=56 * 1024 * 1024),
        name="store",
    )(*results)


def solution(mesh):
    pieces = P(("grp", "dom", "lvl", "sub"), None)
    flat = P(("grp", "dom", "lvl", "sub"))
    return jax.shard_map(
        functools.partial(on_device, mesh.shape["dom"], mesh.shape["lvl"]),
        mesh=mesh,
        in_specs=(
            pieces,
            pieces,
            pieces,
            P(),
            P(),
            P(),
            pieces,
            pieces,
            P("grp", None),
            flat,
            flat,
        ),
        out_specs=(pieces, pieces, pieces),
        check_vma=False,
    )
```

```python
import functools

import jax
import jax.numpy as jnp
from jax import lax
from jax.experimental import pallas as pl
from jax.experimental.pallas import tpu as pltpu
from jax.sharding import PartitionSpec as P

BLOCK = 128
STEP = 384
MESH = pl.DeviceIdType.MESH


def gate(values):
    return 0.5 * jnp.tanh(0.5 * values) + 0.5


def dot(left, right, left_dim=1, right_dim=0):
    return lax.dot_general(
        left, right, (((left_dim,), (right_dim,)), ((), ())), preferred_element_type=jnp.float32
    )


def layer_kernel(
    n_dom,
    n_lvl,
    node_hbm,
    coarse_hbm,
    cot_hbm,
    w_message_hbm,
    w_coarse_hbm,
    w_update_hbm,
    words_hbm,
    tile_hbm,
    partner_hbm,
    assign_hbm,
    live_hbm,
    updated_hbm,
    d_nodes_hbm,
    d_coarse_hbm,
    node,
    coarse,
    cot,
    w_message,
    w_coarse,
    w_update,
    words,
    tile,
    partner,
    assign,
    live,
    adj_back,
    adj_fore,
    spread,
    gather,
    reach,
    echo,
    reach_crs,
    picker,
    pick_back,
    message,
    slope_msg,
    slope_crs,
    aggregate,
    d_agg,
    d_pre,
    updated,
    d_nodes,
    d_coarse,
    send_one,
    land_one,
    send_two,
    land_two,
    coarse_all,
    d_own,
    d_send,
    d_land,
    in_sem,
    out_sem,
    send_sem,
    one_sem,
    two_sem,
    crs_send_sem,
    crs_sem,
    grad_send_sem,
    grad_sem,
):
    rows, hidden = node.shape
    blocks = rows // BLOCK
    c_rows = coarse.shape[0]
    rounds, width = tile.shape
    tiles = n_dom * width
    me = lax.axis_index("dom")
    level = lax.axis_index("lvl")
    doms = [lax.rem(me + step, n_dom) for step in range(1, n_dom)]
    lvls = [lax.rem(level + step, n_lvl) for step in range(1, n_lvl)]

    barrier = pltpu.get_barrier_semaphore()
    for other in doms:
        pl.semaphore_signal(barrier, inc=1, device_id={"dom": other}, device_id_type=MESH)
    for other in lvls:
        pl.semaphore_signal(barrier, inc=1, device_id={"lvl": other}, device_id_type=MESH)

    pairs = dict(
        tile=(tile_hbm, tile),
        partner=(partner_hbm, partner),
        live=(live_hbm, live),
        words=(words_hbm, words),
        assign=(assign_hbm, assign),
        node=(node_hbm, node),
        w_message=(w_message_hbm, w_message),
        coarse=(coarse_hbm, coarse),
        w_coarse=(w_coarse_hbm, w_coarse),
        w_update=(w_update_hbm, w_update),
        cot=(cot_hbm, cot),
    )
    loads = {
        name: pltpu.make_async_copy(pair[0], pair[1], in_sem.at[i])
        for i, (name, pair) in enumerate(pairs.items())
    }
    for load in loads.values():
        load.start()

    def trade(source, landing, landing_sem, base):
        own = pl.ds(pl.multiple_of(me * width, width), width)
        copies = []
        for i, other in enumerate(doms):
            copy = pltpu.make_async_remote_copy(
                src_ref=source.at[pl.ds(pl.multiple_of(other * width, width), width)],
                dst_ref=landing.at[own],
                send_sem=send_sem.at[base + i],
                recv_sem=landing_sem.at[i],
                device_id={"dom": other},
                device_id_type=MESH,
            )
            copy.start()
            copies.append(copy)
        landing[own, :] = source[own, :]
        return copies

    loads["tile"].wait()
    loads["partner"].wait()
    loads["live"].wait()
    count = live[0]
    peer_of = lax.broadcasted_iota(jnp.int32, (1, tiles), 1) // width
    target = jnp.full((1, tiles), -1, jnp.int32)
    for r in range(rounds):
        wide = jnp.concatenate([tile[r : r + 1, :]] * n_dom, axis=1)
        target = jnp.where(peer_of == partner[r, me], wide, target)
    place = lax.broadcasted_iota(jnp.int32, (rows, tiles), 0)
    spread_f = jnp.where(place == target, 1.0, 0.0)
    spread[...] = spread_f.astype(jnp.bfloat16)
    gather_f = jnp.transpose(spread_f)
    gather[...] = gather_f.astype(jnp.bfloat16)
    lane = lax.broadcasted_iota(jnp.int32, (tiles, rows), 1)
    live_t = jnp.sum(jnp.where(lane < count, gather_f, 0.0), axis=1, keepdims=True)

    loads["words"].wait()
    loads["assign"].wait()
    bits = jnp.concatenate(
        [jnp.broadcast_to(words[w : w + 1, :], (16, rows)) for w in range(BLOCK // 16)], axis=0
    )
    shift = lax.broadcasted_iota(jnp.int32, (BLOCK, rows), 0) % 16
    bits = jnp.bitwise_and(jnp.right_shift(bits, shift), 1)
    adj_f = 0.125 * bits.astype(jnp.float32)
    adj_back[...] = adj_f.astype(jnp.bfloat16)
    adj_fore[...] = jnp.transpose(adj_f).astype(jnp.bfloat16)
    coarse_at = lax.broadcasted_iota(jnp.int32, (n_lvl * c_rows, rows), 0)
    pick_f = jnp.where(coarse_at == assign[...].reshape(1, rows), 1.0, 0.0)
    pick_back[...] = pick_f.astype(jnp.bfloat16)
    picker[...] = jnp.transpose(pick_f).astype(jnp.bfloat16)
    for b in range(blocks):
        part = pl.ds(b * BLOCK, BLOCK)
        reach[:, part] = dot(gather[:, part], adj_fore[part, :]).astype(jnp.bfloat16)
    echo[...] = dot(gather[...], spread[...]).astype(jnp.bfloat16)
    reach_crs[...] = dot(gather[...], picker[...]).astype(jnp.bfloat16)

    loads["node"].wait()
    loads["w_message"].wait()
    node_t = dot(gather[...], node[...]).astype(jnp.bfloat16)
    pre_t = dot(node_t, w_message[...])
    send_one[...] = (live_t * (pre_t * gate(pre_t))).astype(jnp.bfloat16)
    pl.semaphore_wait(barrier, n_dom - 1 + n_lvl - 1)
    sent = trade(send_one, land_one, one_sem, 0)

    loads["coarse"].wait()
    loads["w_coarse"].wait()
    pre_crs = dot(coarse[...], w_coarse[...])
    gate_crs = gate(pre_crs)
    silu_crs = pre_crs * gate_crs
    slope_crs[...] = gate_crs + silu_crs * (1.0 - gate_crs)
    own_crs = pl.ds(pl.multiple_of(level * c_rows, c_rows), c_rows)
    coarse_all[own_crs, :] = silu_crs.astype(jnp.bfloat16)
    crs_copies = []
    for i, other in enumerate(lvls):
        copy = pltpu.make_async_remote_copy(
            src_ref=coarse_all.at[own_crs],
            dst_ref=coarse_all.at[own_crs],
            send_sem=crs_send_sem.at[i],
            recv_sem=crs_sem.at[i],
            device_id={"lvl": other},
            device_id_type=MESH,
        )
        copy.start()
        crs_copies.append(copy)

    def live_rows(start):
        at = lax.broadcasted_iota(jnp.int32, (STEP, hidden), 0) + start
        return at < count

    for start in range(0, rows, STEP):
        part = pl.ds(start, STEP)
        pre = dot(node[part, :], w_message[...])
        g = gate(pre)
        silu = pre * g
        alive = live_rows(start)
        message[part, :] = jnp.where(alive, silu, 0.0).astype(jnp.bfloat16)
        slope_msg[part, :] = jnp.where(alive, g + silu * (1.0 - g), 0.0)

    loads["cot"].wait()
    cot_t = dot(gather[...], cot[...])

    for copy in sent:
        copy.wait_recv()
    for copy in crs_copies:
        copy.wait_recv()

    loads["w_update"].wait()
    agg_t = dot(reach[...], message[...])
    agg_t += dot(reach_crs[...], coarse_all[...])
    agg_t = (agg_t + dot(echo[...], land_one[...])).astype(jnp.bfloat16)
    pre_t = dot(agg_t, w_update[...])
    g = gate(pre_t)
    d_t = (live_t * cot_t * (g * (1.0 + pre_t * (1.0 - g)))).astype(jnp.bfloat16)
    send_two[...] = dot(d_t, w_update[...], 1, 1).astype(jnp.bfloat16)
    sent_two = trade(send_two, land_two, two_sem, n_dom - 1)

    for b in range(blocks):
        part = pl.ds(b * BLOCK, BLOCK)
        total = dot(adj_fore[part, :], message[part, :])
        total += dot(spread[part, :], land_one[...])
        total += dot(picker[part, :], coarse_all[...])
        aggregate[part, :] = total.astype(jnp.bfloat16)

    for start in range(0, rows, STEP):
        part = pl.ds(start, STEP)
        pre = dot(aggregate[part, :], w_update[...])
        g = gate(pre)
        silu = pre * g
        alive = live_rows(start)
        slope = g + silu * (1.0 - g)
        updated[part, :] = (
            node[part, :].astype(jnp.float32) + jnp.where(alive, silu, 0.0)
        ).astype(jnp.bfloat16)
        d_pre[part, :] = jnp.where(alive, cot[part, :].astype(jnp.float32) * slope, 0.0).astype(
            jnp.bfloat16
        )
        d_agg[part, :] = dot(d_pre[part, :], w_update[...], 1, 1).astype(jnp.bfloat16)

    stores = [pltpu.make_async_copy(updated, updated_hbm, out_sem.at[0])]
    stores[0].start()

    d_own[...] = dot(pick_back[...], d_agg[...])
    d_send[...] = d_own[...].astype(jnp.bfloat16)
    grad_copies = []
    for i, other in enumerate(lvls):
        copy = pltpu.make_async_remote_copy(
            src_ref=d_send.at[pl.ds(pl.multiple_of(other * c_rows, c_rows), c_rows)],
            dst_ref=d_land.at[i],
            send_sem=grad_send_sem.at[i],
            recv_sem=grad_sem.at[i],
            device_id={"lvl": other},
            device_id_type=MESH,
        )
        copy.start()
        grad_copies.append(copy)

    for copy in sent_two:
        copy.wait_recv()
    for start in range(0, rows, STEP):
        for b in range(start // BLOCK, (start + STEP) // BLOCK):
            part = pl.ds(b * BLOCK, BLOCK)
            total = dot(adj_back[:, part], d_agg[part, :])
            total += dot(spread[part, :], land_two[...])
            d_pre[part, :] = (total * slope_msg[part, :]).astype(jnp.bfloat16)
        part = pl.ds(start, STEP)
        d_nodes[part, :] = (
            cot[part, :].astype(jnp.float32) + dot(d_pre[part, :], w_message[...], 1, 1)
        ).astype(jnp.bfloat16)
        stores.append(
            pltpu.make_async_copy(
                d_nodes.at[part], d_nodes_hbm.at[part], out_sem.at[2 + start // STEP]
            )
        )
        stores[-1].start()

    total = d_own[own_crs, :]
    for i, copy in enumerate(grad_copies):
        copy.wait_recv()
        total += d_land[i].astype(jnp.float32)
    d_pre_crs = (total * slope_crs[...]).astype(jnp.bfloat16)
    d_coarse[...] = dot(d_pre_crs, w_coarse[...], 1, 1).astype(jnp.bfloat16)

    stores.append(pltpu.make_async_copy(d_coarse, d_coarse_hbm, out_sem.at[1]))
    stores[-1].start()
    for copy in sent + crs_copies + sent_two + grad_copies:
        copy.wait_send()
    for store in stores:
        store.wait()


def store_kernel(updated, d_nodes, d_coarse, *refs):
    outs, stages, in_sem, out_sem = refs[:3], refs[3:6], refs[6], refs[7]
    parts = []
    for i, ref in enumerate((updated, d_nodes, d_coarse)):
        rows = ref.shape[0]
        step = min(rows, 256)
        parts += [(i, pl.ds(start, step)) for start in range(0, rows, step)]
    sources = (updated, d_nodes, d_coarse)
    loads = [
        pltpu.make_async_copy(sources[i].at[at], stages[i].at[at], in_sem.at[n])
        for n, (i, at) in enumerate(parts)
    ]
    stores = [
        pltpu.make_async_copy(stages[i].at[at], outs[i].at[at], out_sem.at[n])
        for n, (i, at) in enumerate(parts)
    ]
    for load in loads:
        load.start()
    for load, store in zip(loads, stores):
        load.wait()
        store.start()
    for store in stores:
        store.wait()


def on_device(
    n_dom,
    n_lvl,
    node_latents,
    coarse_latents,
    cotangent,
    w_message,
    w_coarse,
    w_update,
    mask_words,
    tile_index,
    partner,
    assignment,
    live_counts,
):
    rows, hidden = node_latents.shape
    c_rows = coarse_latents.shape[0]
    rounds, width = tile_index.shape
    tiles = n_dom * width
    group = n_lvl * c_rows
    bf16, f32, i32 = jnp.bfloat16, jnp.float32, jnp.int32
    vmem = pltpu.VMEM
    dma = pltpu.SemaphoreType.DMA
    scratch = [
        vmem((rows, hidden), bf16),
        vmem((c_rows, hidden), bf16),
        vmem((rows, hidden), bf16),
        vmem((hidden, hidden), bf16),
        vmem((hidden, hidden), bf16),
        vmem((hidden, hidden), bf16),
        vmem((8, rows), i32),
        vmem((rounds, width), i32),
        pltpu.SMEM((rounds, n_dom), i32),
        vmem((rows,), i32),
        pltpu.SMEM((1,), i32),
        vmem((BLOCK, rows), bf16),
        vmem((rows, BLOCK), bf16),
        vmem((rows, tiles), bf16),
        vmem((tiles, rows), bf16),
        vmem((tiles, rows), bf16),
        vmem((tiles, tiles), bf16),
        vmem((tiles, group), bf16),
        vmem((rows, group), bf16),
        vmem((group, rows), bf16),
        vmem((rows, hidden), bf16),
        vmem((rows, hidden), f32),
        vmem((c_rows, hidden), f32),
        vmem((rows, hidden), bf16),
        vmem((rows, hidden), bf16),
        vmem((rows, hidden), bf16),
        vmem((rows, hidden), bf16),
        vmem((rows, hidden), bf16),
        vmem((c_rows, hidden), bf16),
        vmem((tiles, hidden), bf16),
        vmem((tiles, hidden), bf16),
        vmem((tiles, hidden), bf16),
        vmem((tiles, hidden), bf16),
        vmem((group, hidden), bf16),
        vmem((group, hidden), f32),
        vmem((group, hidden), bf16),
        vmem((n_lvl - 1, c_rows, hidden), bf16),
        dma((11,)),
        dma((2 + rows // STEP,)),
        dma((2 * (n_dom - 1),)),
        dma((n_dom - 1,)),
        dma((n_dom - 1,)),
        dma((n_lvl - 1,)),
        dma((n_lvl - 1,)),
        dma((n_lvl - 1,)),
        dma((n_lvl - 1,)),
    ]
    far = pl.BlockSpec(memory_space=pl.ANY)
    outs = (
        jax.ShapeDtypeStruct((rows, hidden), bf16),
        jax.ShapeDtypeStruct((rows, hidden), bf16),
        jax.ShapeDtypeStruct((c_rows, hidden), bf16),
    )
    results = pl.pallas_call(
        functools.partial(layer_kernel, n_dom, n_lvl),
        out_shape=outs,
        in_specs=[far] * 11,
        out_specs=(far,) * 3,
        scratch_shapes=scratch,
        compiler_params=pltpu.CompilerParams(
            collective_id=0, has_side_effects=True, vmem_limit_bytes=56 * 1024 * 1024
        ),
        name="layer",
    )(
        node_latents,
        coarse_latents,
        cotangent,
        w_message,
        w_coarse,
        w_update,
        jnp.transpose(mask_words),
        tile_index,
        partner,
        assignment,
        live_counts,
    )
    return pl.pallas_call(
        store_kernel,
        out_shape=outs,
        in_specs=[far] * 3,
        out_specs=(far,) * 3,
        scratch_shapes=[vmem(out.shape, bf16) for out in outs] + [dma((7,)), dma((7,))],
        compiler_params=pltpu.CompilerParams(vmem_limit_bytes=56 * 1024 * 1024),
        name="store",
    )(*results)


def solution(mesh):
    pieces = P(("grp", "dom", "lvl", "sub"), None)
    flat = P(("grp", "dom", "lvl", "sub"))
    return jax.shard_map(
        functools.partial(on_device, mesh.shape["dom"], mesh.shape["lvl"]),
        mesh=mesh,
        in_specs=(
            pieces,
            pieces,
            pieces,
            P(),
            P(),
            P(),
            pieces,
            pieces,
            P("grp", None),
            flat,
            flat,
        ),
        out_specs=(pieces, pieces, pieces),
        check_vma=False,
    )
```

```python
import functools

import jax
import jax.numpy as jnp
from jax import lax
from jax.experimental import pallas as pl
from jax.experimental.pallas import tpu as pltpu
from jax.sharding import PartitionSpec as P

BLOCK = 128
STEP = 384
MESH = pl.DeviceIdType.MESH


def gate(values):
    return 0.5 * jnp.tanh(0.5 * values) + 0.5


def dot(left, right, left_dim=1, right_dim=0):
    return lax.dot_general(
        left, right, (((left_dim,), (right_dim,)), ((), ())), preferred_element_type=jnp.float32
    )


def layer_kernel(
    n_dom,
    n_lvl,
    node_hbm,
    coarse_hbm,
    cot_hbm,
    w_message_hbm,
    w_coarse_hbm,
    w_update_hbm,
    words_hbm,
    tile_hbm,
    partner_hbm,
    assign_hbm,
    live_hbm,
    updated_hbm,
    d_nodes_hbm,
    d_coarse_hbm,
    node,
    coarse,
    cot,
    w_message,
    w_coarse,
    w_update,
    words,
    tile,
    partner,
    assign,
    live,
    adj_back,
    adj_fore,
    spread,
    gather,
    reach,
    reach_far,
    far_fore,
    pick_back,
    message,
    slope_msg,
    slope_crs,
    near,
    aggregate,
    d_agg,
    d_pre,
    updated,
    d_nodes,
    d_coarse,
    send_one,
    send_two,
    land_two,
    landed,
    d_own,
    d_send,
    d_land,
    in_sem,
    out_sem,
    send_sem,
    one_sem,
    two_sem,
    crs_send_sem,
    crs_sem,
    grad_send_sem,
    grad_sem,
):
    rows, hidden = node.shape
    blocks = rows // BLOCK
    c_rows = coarse.shape[0]
    rounds, width = tile.shape
    tiles = n_dom * width
    me = lax.axis_index("dom")
    level = lax.axis_index("lvl")
    doms = [lax.rem(me + step, n_dom) for step in range(1, n_dom)]
    lvls = [lax.rem(level + step, n_lvl) for step in range(1, n_lvl)]

    barrier = pltpu.get_barrier_semaphore()
    for other in doms:
        pl.semaphore_signal(barrier, inc=1, device_id={"dom": other}, device_id_type=MESH)
    for other in lvls:
        pl.semaphore_signal(barrier, inc=1, device_id={"lvl": other}, device_id_type=MESH)

    pairs = dict(
        tile=(tile_hbm, tile),
        partner=(partner_hbm, partner),
        live=(live_hbm, live),
        words=(words_hbm, words),
        assign=(assign_hbm, assign),
        node=(node_hbm, node),
        w_message=(w_message_hbm, w_message),
        coarse=(coarse_hbm, coarse),
        w_coarse=(w_coarse_hbm, w_coarse),
        w_update=(w_update_hbm, w_update),
        cot=(cot_hbm, cot),
    )
    loads = {
        name: pltpu.make_async_copy(pair[0], pair[1], in_sem.at[i])
        for i, (name, pair) in enumerate(pairs.items())
    }
    for load in loads.values():
        load.start()

    def trade(source, landing, landing_sem, base):
        own = pl.ds(pl.multiple_of(me * width, width), width)
        copies = []
        for i, other in enumerate(doms):
            copy = pltpu.make_async_remote_copy(
                src_ref=source.at[pl.ds(pl.multiple_of(other * width, width), width)],
                dst_ref=landing.at[own],
                send_sem=send_sem.at[base + i],
                recv_sem=landing_sem.at[i],
                device_id={"dom": other},
                device_id_type=MESH,
            )
            copy.start()
            copies.append(copy)
        landing[own, :] = source[own, :]
        return copies

    loads["tile"].wait()
    loads["partner"].wait()
    loads["live"].wait()
    count = live[0]
    peer_of = lax.broadcasted_iota(jnp.int32, (1, tiles), 1) // width
    target = jnp.full((1, tiles), -1, jnp.int32)
    for r in range(rounds):
        wide = jnp.concatenate([tile[r : r + 1, :]] * n_dom, axis=1)
        target = jnp.where(peer_of == partner[r, me], wide, target)
    place = lax.broadcasted_iota(jnp.int32, (rows, tiles), 0)
    spread_f = jnp.where(place == target, 1.0, 0.0)
    spread[...] = spread_f.astype(jnp.bfloat16)
    gather_f = jnp.transpose(spread_f)
    gather[...] = gather_f.astype(jnp.bfloat16)
    lane = lax.broadcasted_iota(jnp.int32, (tiles, rows), 1)
    live_t = jnp.sum(jnp.where(lane < count, gather_f, 0.0), axis=1, keepdims=True)

    loads["node"].wait()
    loads["w_message"].wait()
    node_t = dot(gather[...], node[...]).astype(jnp.bfloat16)
    pre_t = dot(node_t, w_message[...])
    send_one[...] = (live_t * (pre_t * gate(pre_t))).astype(jnp.bfloat16)
    pl.semaphore_wait(barrier, n_dom - 1 + n_lvl - 1)
    sent = trade(send_one, landed, one_sem, 0)

    loads["coarse"].wait()
    loads["w_coarse"].wait()
    pre_crs = dot(coarse[...], w_coarse[...])
    gate_crs = gate(pre_crs)
    silu_crs = pre_crs * gate_crs
    slope_crs[...] = gate_crs + silu_crs * (1.0 - gate_crs)
    own_crs = pl.ds(pl.multiple_of(level * c_rows, c_rows), c_rows)
    own_far = pl.ds(pl.multiple_of(tiles + level * c_rows, c_rows), c_rows)
    landed[own_far, :] = silu_crs.astype(jnp.bfloat16)
    crs_copies = []
    for i, other in enumerate(lvls):
        copy = pltpu.make_async_remote_copy(
            src_ref=landed.at[own_far],
            dst_ref=landed.at[own_far],
            send_sem=crs_send_sem.at[i],
            recv_sem=crs_sem.at[i],
            device_id={"lvl": other},
            device_id_type=MESH,
        )
        copy.start()
        crs_copies.append(copy)

    loads["words"].wait()
    loads["assign"].wait()
    bits = jnp.concatenate(
        [jnp.broadcast_to(words[w : w + 1, :], (16, rows)) for w in range(BLOCK // 16)], axis=0
    )
    shift = lax.broadcasted_iota(jnp.int32, (BLOCK, rows), 0) % 16
    bits = jnp.bitwise_and(jnp.right_shift(bits, shift), 1)
    adj_f = 0.125 * bits.astype(jnp.float32)
    adj_back[...] = adj_f.astype(jnp.bfloat16)
    adj_fore[...] = jnp.transpose(adj_f).astype(jnp.bfloat16)
    coarse_at = lax.broadcasted_iota(jnp.int32, (n_lvl * c_rows, rows), 0)
    pick_f = jnp.where(coarse_at == assign[...].reshape(1, rows), 1.0, 0.0)
    pick_back[...] = pick_f.astype(jnp.bfloat16)
    far_fore[...] = jnp.concatenate([spread_f, jnp.transpose(pick_f)], axis=1).astype(jnp.bfloat16)
    for b in range(blocks):
        part = pl.ds(b * BLOCK, BLOCK)
        reach[:, part] = dot(gather[:, part], adj_fore[part, :]).astype(jnp.bfloat16)
    reach_far[...] = dot(gather[...], far_fore[...]).astype(jnp.bfloat16)

    def live_rows(start):
        at = lax.broadcasted_iota(jnp.int32, (STEP, hidden), 0) + start
        return at < count

    for start in range(0, rows, STEP):
        part = pl.ds(start, STEP)
        pre = dot(node[part, :], w_message[...])
        g = gate(pre)
        silu = pre * g
        alive = live_rows(start)
        message[part, :] = jnp.where(alive, silu, 0.0).astype(jnp.bfloat16)
        slope_msg[part, :] = jnp.where(alive, g + silu * (1.0 - g), 0.0)

    loads["cot"].wait()
    cot_t = dot(gather[...], cot[...])

    for b in range(blocks):
        part = pl.ds(b * BLOCK, BLOCK)
        near[part, :] = dot(adj_fore[part, :], message[part, :])
    for copy in sent:
        copy.wait_recv()
    for copy in crs_copies:
        copy.wait_recv()

    loads["w_update"].wait()
    agg_t = dot(reach[...], message[...])
    agg_t = (agg_t + dot(reach_far[...], landed[...])).astype(jnp.bfloat16)
    pre_t = dot(agg_t, w_update[...])
    g = gate(pre_t)
    d_t = (live_t * cot_t * (g * (1.0 + pre_t * (1.0 - g)))).astype(jnp.bfloat16)
    send_two[...] = dot(d_t, w_update[...], 1, 1).astype(jnp.bfloat16)
    sent_two = trade(send_two, land_two, two_sem, n_dom - 1)

    for b in range(blocks):
        part = pl.ds(b * BLOCK, BLOCK)
        total = near[part, :] + dot(far_fore[part, :], landed[...])
        aggregate[part, :] = total.astype(jnp.bfloat16)

    for start in range(0, rows, STEP):
        part = pl.ds(start, STEP)
        pre = dot(aggregate[part, :], w_update[...])
        g = gate(pre)
        silu = pre * g
        alive = live_rows(start)
        slope = g + silu * (1.0 - g)
        updated[part, :] = (
            node[part, :].astype(jnp.float32) + jnp.where(alive, silu, 0.0)
        ).astype(jnp.bfloat16)
        d_pre[part, :] = jnp.where(alive, cot[part, :].astype(jnp.float32) * slope, 0.0).astype(
            jnp.bfloat16
        )
        d_agg[part, :] = dot(d_pre[part, :], w_update[...], 1, 1).astype(jnp.bfloat16)

    stores = [pltpu.make_async_copy(updated, updated_hbm, out_sem.at[0])]
    stores[0].start()

    d_own[...] = dot(pick_back[...], d_agg[...])
    d_send[...] = d_own[...].astype(jnp.bfloat16)
    grad_copies = []
    for i, other in enumerate(lvls):
        copy = pltpu.make_async_remote_copy(
            src_ref=d_send.at[pl.ds(pl.multiple_of(other * c_rows, c_rows), c_rows)],
            dst_ref=d_land.at[i],
            send_sem=grad_send_sem.at[i],
            recv_sem=grad_sem.at[i],
            device_id={"lvl": other},
            device_id_type=MESH,
        )
        copy.start()
        grad_copies.append(copy)

    for copy in sent_two:
        copy.wait_recv()
    for start in range(0, rows, STEP):
        for b in range(start // BLOCK, (start + STEP) // BLOCK):
            part = pl.ds(b * BLOCK, BLOCK)
            total = dot(adj_back[:, part], d_agg[part, :])
            total += dot(spread[part, :], land_two[...])
            d_pre[part, :] = (total * slope_msg[part, :]).astype(jnp.bfloat16)
        part = pl.ds(start, STEP)
        d_nodes[part, :] = (
            cot[part, :].astype(jnp.float32) + dot(d_pre[part, :], w_message[...], 1, 1)
        ).astype(jnp.bfloat16)
        stores.append(
            pltpu.make_async_copy(
                d_nodes.at[part], d_nodes_hbm.at[part], out_sem.at[2 + start // STEP]
            )
        )
        stores[-1].start()

    total = d_own[own_crs, :]
    for i, copy in enumerate(grad_copies):
        copy.wait_recv()
        total += d_land[i].astype(jnp.float32)
    d_pre_crs = (total * slope_crs[...]).astype(jnp.bfloat16)
    d_coarse[...] = dot(d_pre_crs, w_coarse[...], 1, 1).astype(jnp.bfloat16)

    stores.append(pltpu.make_async_copy(d_coarse, d_coarse_hbm, out_sem.at[1]))
    stores[-1].start()
    for copy in sent + crs_copies + sent_two + grad_copies:
        copy.wait_send()
    for store in stores:
        store.wait()


def store_kernel(updated, d_nodes, d_coarse, *refs):
    outs, stages, in_sem, out_sem = refs[:3], refs[3:6], refs[6], refs[7]
    parts = []
    for i, ref in enumerate((updated, d_nodes, d_coarse)):
        rows = ref.shape[0]
        step = min(rows, 256)
        parts += [(i, pl.ds(start, step)) for start in range(0, rows, step)]
    sources = (updated, d_nodes, d_coarse)
    loads = [
        pltpu.make_async_copy(sources[i].at[at], stages[i].at[at], in_sem.at[n])
        for n, (i, at) in enumerate(parts)
    ]
    stores = [
        pltpu.make_async_copy(stages[i].at[at], outs[i].at[at], out_sem.at[n])
        for n, (i, at) in enumerate(parts)
    ]
    for load in loads:
        load.start()
    for load, store in zip(loads, stores):
        load.wait()
        store.start()
    for store in stores:
        store.wait()


def on_device(
    n_dom,
    n_lvl,
    node_latents,
    coarse_latents,
    cotangent,
    w_message,
    w_coarse,
    w_update,
    mask_words,
    tile_index,
    partner,
    assignment,
    live_counts,
):
    rows, hidden = node_latents.shape
    c_rows = coarse_latents.shape[0]
    rounds, width = tile_index.shape
    tiles = n_dom * width
    group = n_lvl * c_rows
    bf16, f32, i32 = jnp.bfloat16, jnp.float32, jnp.int32
    vmem = pltpu.VMEM
    dma = pltpu.SemaphoreType.DMA
    scratch = [
        vmem((rows, hidden), bf16),
        vmem((c_rows, hidden), bf16),
        vmem((rows, hidden), bf16),
        vmem((hidden, hidden), bf16),
        vmem((hidden, hidden), bf16),
        vmem((hidden, hidden), bf16),
        vmem((8, rows), i32),
        vmem((rounds, width), i32),
        pltpu.SMEM((rounds, n_dom), i32),
        vmem((rows,), i32),
        pltpu.SMEM((1,), i32),
        vmem((BLOCK, rows), bf16),
        vmem((rows, BLOCK), bf16),
        vmem((rows, tiles), bf16),
        vmem((tiles, rows), bf16),
        vmem((tiles, rows), bf16),
        vmem((tiles, tiles + group), bf16),
        vmem((rows, tiles + group), bf16),
        vmem((group, rows), bf16),
        vmem((rows, hidden), bf16),
        vmem((rows, hidden), f32),
        vmem((c_rows, hidden), f32),
        vmem((rows, hidden), f32),
        vmem((rows, hidden), bf16),
        vmem((rows, hidden), bf16),
        vmem((rows, hidden), bf16),
        vmem((rows, hidden), bf16),
        vmem((rows, hidden), bf16),
        vmem((c_rows, hidden), bf16),
        vmem((tiles, hidden), bf16),
        vmem((tiles, hidden), bf16),
        vmem((tiles, hidden), bf16),
        vmem((tiles + group, hidden), bf16),
        vmem((group, hidden), f32),
        vmem((group, hidden), bf16),
        vmem((n_lvl - 1, c_rows, hidden), bf16),
        dma((11,)),
        dma((2 + rows // STEP,)),
        dma((2 * (n_dom - 1),)),
        dma((n_dom - 1,)),
        dma((n_dom - 1,)),
        dma((n_lvl - 1,)),
        dma((n_lvl - 1,)),
        dma((n_lvl - 1,)),
        dma((n_lvl - 1,)),
    ]
    far = pl.BlockSpec(memory_space=pl.ANY)
    outs = (
        jax.ShapeDtypeStruct((rows, hidden), bf16),
        jax.ShapeDtypeStruct((rows, hidden), bf16),
        jax.ShapeDtypeStruct((c_rows, hidden), bf16),
    )
    results = pl.pallas_call(
        functools.partial(layer_kernel, n_dom, n_lvl),
        out_shape=outs,
        in_specs=[far] * 11,
        out_specs=(far,) * 3,
        scratch_shapes=scratch,
        compiler_params=pltpu.CompilerParams(
            collective_id=0, has_side_effects=True, vmem_limit_bytes=56 * 1024 * 1024
        ),
        name="layer",
    )(
        node_latents,
        coarse_latents,
        cotangent,
        w_message,
        w_coarse,
        w_update,
        jnp.transpose(mask_words),
        tile_index,
        partner,
        assignment,
        live_counts,
    )
    return pl.pallas_call(
        store_kernel,
        out_shape=outs,
        in_specs=[far] * 3,
        out_specs=(far,) * 3,
        scratch_shapes=[vmem(out.shape, bf16) for out in outs] + [dma((7,)), dma((7,))],
        compiler_params=pltpu.CompilerParams(vmem_limit_bytes=56 * 1024 * 1024),
        name="store",
    )(*results)


def solution(mesh):
    pieces = P(("grp", "dom", "lvl", "sub"), None)
    flat = P(("grp", "dom", "lvl", "sub"))
    return jax.shard_map(
        functools.partial(on_device, mesh.shape["dom"], mesh.shape["lvl"]),
        mesh=mesh,
        in_specs=(
            pieces,
            pieces,
            pieces,
            P(),
            P(),
            P(),
            pieces,
            pieces,
            P("grp", None),
            flat,
            flat,
        ),
        out_specs=(pieces, pieces, pieces),
        check_vma=False,
    )
```

```python
import functools

import jax
import jax.numpy as jnp
from jax import lax
from jax.experimental import pallas as pl
from jax.experimental.pallas import tpu as pltpu
from jax.sharding import PartitionSpec as P

BLOCK = 128
STEP = 384
MESH = pl.DeviceIdType.MESH


def gate(values):
    return 0.5 * jnp.tanh(0.5 * values) + 0.5


def dot(left, right, left_dim=1, right_dim=0):
    return lax.dot_general(
        left, right, (((left_dim,), (right_dim,)), ((), ())), preferred_element_type=jnp.float32
    )


def layer_kernel(
    n_dom,
    n_lvl,
    node_hbm,
    coarse_hbm,
    cot_hbm,
    w_message_hbm,
    w_coarse_hbm,
    w_update_hbm,
    words_hbm,
    tile_hbm,
    partner_hbm,
    assign_hbm,
    live_hbm,
    updated_hbm,
    d_nodes_hbm,
    d_coarse_hbm,
    node,
    coarse,
    cot,
    w_message,
    w_coarse,
    w_update,
    words,
    tile,
    partner,
    assign,
    live,
    adj_back,
    adj_fore,
    spread,
    gather,
    reach,
    reach_far,
    far_fore,
    pick_back,
    message,
    slope_msg,
    slope_crs,
    near,
    aggregate,
    d_agg,
    d_pre,
    updated,
    d_nodes,
    d_coarse,
    send_one,
    send_two,
    land_two,
    landed,
    d_own,
    d_send,
    d_land,
    in_sem,
    out_sem,
    send_sem,
    one_sem,
    two_sem,
    crs_send_sem,
    crs_sem,
    grad_send_sem,
    grad_sem,
):
    rows, hidden = node.shape
    blocks = rows // BLOCK
    c_rows = coarse.shape[0]
    rounds, width = tile.shape
    tiles = n_dom * width
    me = lax.axis_index("dom")
    level = lax.axis_index("lvl")
    doms = [lax.rem(me + step, n_dom) for step in range(1, n_dom)]
    lvls = [lax.rem(level + step, n_lvl) for step in range(1, n_lvl)]

    barrier = pltpu.get_barrier_semaphore()
    for other in doms:
        pl.semaphore_signal(barrier, inc=1, device_id={"dom": other}, device_id_type=MESH)
    for other in lvls:
        pl.semaphore_signal(barrier, inc=1, device_id={"lvl": other}, device_id_type=MESH)

    pairs = dict(
        tile=(tile_hbm, tile),
        partner=(partner_hbm, partner),
        live=(live_hbm, live),
        words=(words_hbm, words),
        assign=(assign_hbm, assign),
        node=(node_hbm, node),
        w_message=(w_message_hbm, w_message),
        coarse=(coarse_hbm, coarse),
        w_coarse=(w_coarse_hbm, w_coarse),
        w_update=(w_update_hbm, w_update),
        cot=(cot_hbm, cot),
    )
    loads = {
        name: pltpu.make_async_copy(pair[0], pair[1], in_sem.at[i])
        for i, (name, pair) in enumerate(pairs.items())
    }
    for load in loads.values():
        load.start()

    def trade(source, landing, landing_sem, base):
        own = pl.ds(pl.multiple_of(me * width, width), width)
        copies = []
        for i, other in enumerate(doms):
            copy = pltpu.make_async_remote_copy(
                src_ref=source.at[pl.ds(pl.multiple_of(other * width, width), width)],
                dst_ref=landing.at[own],
                send_sem=send_sem.at[base + i],
                recv_sem=landing_sem.at[i],
                device_id={"dom": other},
                device_id_type=MESH,
            )
            copy.start()
            copies.append(copy)
        landing[own, :] = source[own, :]
        return copies

    loads["tile"].wait()
    loads["partner"].wait()
    loads["live"].wait()
    count = live[0]
    peer_of = lax.broadcasted_iota(jnp.int32, (1, tiles), 1) // width
    target = jnp.full((1, tiles), -1, jnp.int32)
    for r in range(rounds):
        wide = jnp.concatenate([tile[r : r + 1, :]] * n_dom, axis=1)
        target = jnp.where(peer_of == partner[r, me], wide, target)
    place = lax.broadcasted_iota(jnp.int32, (rows, tiles), 0)
    spread_f = jnp.where(place == target, 1.0, 0.0)
    spread[...] = spread_f.astype(jnp.bfloat16)
    gather_f = jnp.transpose(spread_f)
    gather[...] = gather_f.astype(jnp.bfloat16)
    lane = lax.broadcasted_iota(jnp.int32, (tiles, rows), 1)
    live_t = jnp.sum(jnp.where(lane < count, gather_f, 0.0), axis=1, keepdims=True)

    loads["node"].wait()
    loads["w_message"].wait()
    node_t = dot(gather[...], node[...]).astype(jnp.bfloat16)
    pre_t = dot(node_t, w_message[...])
    send_one[...] = (live_t * (pre_t * gate(pre_t))).astype(jnp.bfloat16)
    pl.semaphore_wait(barrier, n_dom - 1 + n_lvl - 1)
    sent = trade(send_one, landed, one_sem, 0)

    loads["coarse"].wait()
    loads["w_coarse"].wait()
    pre_crs = dot(coarse[...], w_coarse[...])
    gate_crs = gate(pre_crs)
    silu_crs = pre_crs * gate_crs
    slope_crs[...] = gate_crs + silu_crs * (1.0 - gate_crs)
    own_crs = pl.ds(pl.multiple_of(level * c_rows, c_rows), c_rows)
    own_far = pl.ds(pl.multiple_of(tiles + level * c_rows, c_rows), c_rows)
    landed[own_far, :] = silu_crs.astype(jnp.bfloat16)
    crs_copies = []
    for i, other in enumerate(lvls):
        copy = pltpu.make_async_remote_copy(
            src_ref=landed.at[own_far],
            dst_ref=landed.at[own_far],
            send_sem=crs_send_sem.at[i],
            recv_sem=crs_sem.at[i],
            device_id={"lvl": other},
            device_id_type=MESH,
        )
        copy.start()
        crs_copies.append(copy)

    loads["words"].wait()
    loads["assign"].wait()
    bits = jnp.concatenate(
        [jnp.broadcast_to(words[w : w + 1, :], (16, rows)) for w in range(BLOCK // 16)], axis=0
    )
    shift = lax.broadcasted_iota(jnp.int32, (BLOCK, rows), 0) % 16
    bits = jnp.bitwise_and(jnp.right_shift(bits, shift), 1)
    adj_f = 0.125 * bits.astype(jnp.float32)
    adj_back[...] = adj_f.astype(jnp.bfloat16)
    adj_fore[...] = jnp.transpose(adj_f).astype(jnp.bfloat16)
    coarse_at = lax.broadcasted_iota(jnp.int32, (n_lvl * c_rows, rows), 0)
    pick_f = jnp.where(coarse_at == assign[...].reshape(1, rows), 1.0, 0.0)
    pick_back[...] = pick_f.astype(jnp.bfloat16)
    far_fore[...] = jnp.concatenate([spread_f, jnp.transpose(pick_f)], axis=1).astype(jnp.bfloat16)
    for b in range(blocks):
        part = pl.ds(b * BLOCK, BLOCK)
        reach[:, part] = dot(gather[:, part], adj_fore[part, :]).astype(jnp.bfloat16)
    reach_far[...] = dot(gather[...], far_fore[...]).astype(jnp.bfloat16)

    def live_rows(start):
        at = lax.broadcasted_iota(jnp.int32, (STEP, hidden), 0) + start
        return at < count

    for start in range(0, rows, STEP):
        part = pl.ds(start, STEP)
        pre = dot(node[part, :], w_message[...])
        g = gate(pre)
        silu = pre * g
        alive = live_rows(start)
        message[part, :] = jnp.where(alive, silu, 0.0).astype(jnp.bfloat16)
        slope_msg[part, :] = jnp.where(alive, g + silu * (1.0 - g), 0.0)

    loads["cot"].wait()
    cot_t = dot(gather[...], cot[...])

    for b in range(blocks):
        part = pl.ds(b * BLOCK, BLOCK)
        near[part, :] = dot(adj_fore[part, :], message[part, :])
    for copy in sent:
        copy.wait_recv()
    for copy in crs_copies:
        copy.wait_recv()

    loads["w_update"].wait()
    agg_t = dot(reach[...], message[...])
    agg_t = (agg_t + dot(reach_far[...], landed[...])).astype(jnp.bfloat16)
    pre_t = dot(agg_t, w_update[...])
    g = gate(pre_t)
    d_t = (live_t * cot_t * (g * (1.0 + pre_t * (1.0 - g)))).astype(jnp.bfloat16)
    send_two[...] = dot(d_t, w_update[...], 1, 1).astype(jnp.bfloat16)
    sent_two = trade(send_two, land_two, two_sem, n_dom - 1)

    for b in range(blocks):
        part = pl.ds(b * BLOCK, BLOCK)
        total = near[part, :] + dot(far_fore[part, :], landed[...])
        aggregate[part, :] = total.astype(jnp.bfloat16)

    for start in range(0, rows, STEP):
        part = pl.ds(start, STEP)
        pre = dot(aggregate[part, :], w_update[...])
        g = gate(pre)
        silu = pre * g
        alive = live_rows(start)
        slope = g + silu * (1.0 - g)
        updated[part, :] = (
            node[part, :].astype(jnp.float32) + jnp.where(alive, silu, 0.0)
        ).astype(jnp.bfloat16)
        d_pre[part, :] = jnp.where(alive, cot[part, :].astype(jnp.float32) * slope, 0.0).astype(
            jnp.bfloat16
        )
        d_agg[part, :] = dot(d_pre[part, :], w_update[...], 1, 1).astype(jnp.bfloat16)

    stores = [pltpu.make_async_copy(updated, updated_hbm, out_sem.at[0])]
    stores[0].start()

    d_own[...] = dot(pick_back[...], d_agg[...])
    d_send[...] = d_own[...].astype(jnp.bfloat16)
    grad_copies = []
    for i, other in enumerate(lvls):
        copy = pltpu.make_async_remote_copy(
            src_ref=d_send.at[pl.ds(pl.multiple_of(other * c_rows, c_rows), c_rows)],
            dst_ref=d_land.at[i],
            send_sem=grad_send_sem.at[i],
            recv_sem=grad_sem.at[i],
            device_id={"lvl": other},
            device_id_type=MESH,
        )
        copy.start()
        grad_copies.append(copy)

    for b in range(blocks):
        part = pl.ds(b * BLOCK, BLOCK)
        near[part, :] = dot(adj_back[:, part], d_agg[part, :])
    for copy in sent_two:
        copy.wait_recv()
    for start in range(0, rows, STEP):
        for b in range(start // BLOCK, (start + STEP) // BLOCK):
            part = pl.ds(b * BLOCK, BLOCK)
            total = near[part, :] + dot(spread[part, :], land_two[...])
            d_pre[part, :] = (total * slope_msg[part, :]).astype(jnp.bfloat16)
        part = pl.ds(start, STEP)
        d_nodes[part, :] = (
            cot[part, :].astype(jnp.float32) + dot(d_pre[part, :], w_message[...], 1, 1)
        ).astype(jnp.bfloat16)
        stores.append(
            pltpu.make_async_copy(
                d_nodes.at[part], d_nodes_hbm.at[part], out_sem.at[2 + start // STEP]
            )
        )
        stores[-1].start()

    total = d_own[own_crs, :]
    for i, copy in enumerate(grad_copies):
        copy.wait_recv()
        total += d_land[i].astype(jnp.float32)
    d_pre_crs = (total * slope_crs[...]).astype(jnp.bfloat16)
    d_coarse[...] = dot(d_pre_crs, w_coarse[...], 1, 1).astype(jnp.bfloat16)

    stores.append(pltpu.make_async_copy(d_coarse, d_coarse_hbm, out_sem.at[1]))
    stores[-1].start()
    for copy in sent + crs_copies + sent_two + grad_copies:
        copy.wait_send()
    for store in stores:
        store.wait()


def store_kernel(updated, d_nodes, d_coarse, *refs):
    outs, stages, in_sem, out_sem = refs[:3], refs[3:6], refs[6], refs[7]
    parts = []
    for i, ref in enumerate((updated, d_nodes, d_coarse)):
        rows = ref.shape[0]
        step = min(rows, 256)
        parts += [(i, pl.ds(start, step)) for start in range(0, rows, step)]
    sources = (updated, d_nodes, d_coarse)
    loads = [
        pltpu.make_async_copy(sources[i].at[at], stages[i].at[at], in_sem.at[n])
        for n, (i, at) in enumerate(parts)
    ]
    stores = [
        pltpu.make_async_copy(stages[i].at[at], outs[i].at[at], out_sem.at[n])
        for n, (i, at) in enumerate(parts)
    ]
    for load in loads:
        load.start()
    for load, store in zip(loads, stores):
        load.wait()
        store.start()
    for store in stores:
        store.wait()


def on_device(
    n_dom,
    n_lvl,
    node_latents,
    coarse_latents,
    cotangent,
    w_message,
    w_coarse,
    w_update,
    mask_words,
    tile_index,
    partner,
    assignment,
    live_counts,
):
    rows, hidden = node_latents.shape
    c_rows = coarse_latents.shape[0]
    rounds, width = tile_index.shape
    tiles = n_dom * width
    group = n_lvl * c_rows
    bf16, f32, i32 = jnp.bfloat16, jnp.float32, jnp.int32
    vmem = pltpu.VMEM
    dma = pltpu.SemaphoreType.DMA
    scratch = [
        vmem((rows, hidden), bf16),
        vmem((c_rows, hidden), bf16),
        vmem((rows, hidden), bf16),
        vmem((hidden, hidden), bf16),
        vmem((hidden, hidden), bf16),
        vmem((hidden, hidden), bf16),
        vmem((8, rows), i32),
        vmem((rounds, width), i32),
        pltpu.SMEM((rounds, n_dom), i32),
        vmem((rows,), i32),
        pltpu.SMEM((1,), i32),
        vmem((BLOCK, rows), bf16),
        vmem((rows, BLOCK), bf16),
        vmem((rows, tiles), bf16),
        vmem((tiles, rows), bf16),
        vmem((tiles, rows), bf16),
        vmem((tiles, tiles + group), bf16),
        vmem((rows, tiles + group), bf16),
        vmem((group, rows), bf16),
        vmem((rows, hidden), bf16),
        vmem((rows, hidden), f32),
        vmem((c_rows, hidden), f32),
        vmem((rows, hidden), f32),
        vmem((rows, hidden), bf16),
        vmem((rows, hidden), bf16),
        vmem((rows, hidden), bf16),
        vmem((rows, hidden), bf16),
        vmem((rows, hidden), bf16),
        vmem((c_rows, hidden), bf16),
        vmem((tiles, hidden), bf16),
        vmem((tiles, hidden), bf16),
        vmem((tiles, hidden), bf16),
        vmem((tiles + group, hidden), bf16),
        vmem((group, hidden), f32),
        vmem((group, hidden), bf16),
        vmem((n_lvl - 1, c_rows, hidden), bf16),
        dma((11,)),
        dma((2 + rows // STEP,)),
        dma((2 * (n_dom - 1),)),
        dma((n_dom - 1,)),
        dma((n_dom - 1,)),
        dma((n_lvl - 1,)),
        dma((n_lvl - 1,)),
        dma((n_lvl - 1,)),
        dma((n_lvl - 1,)),
    ]
    far = pl.BlockSpec(memory_space=pl.ANY)
    outs = (
        jax.ShapeDtypeStruct((rows, hidden), bf16),
        jax.ShapeDtypeStruct((rows, hidden), bf16),
        jax.ShapeDtypeStruct((c_rows, hidden), bf16),
    )
    results = pl.pallas_call(
        functools.partial(layer_kernel, n_dom, n_lvl),
        out_shape=outs,
        in_specs=[far] * 11,
        out_specs=(far,) * 3,
        scratch_shapes=scratch,
        compiler_params=pltpu.CompilerParams(
            collective_id=0, has_side_effects=True, vmem_limit_bytes=56 * 1024 * 1024
        ),
        name="layer",
    )(
        node_latents,
        coarse_latents,
        cotangent,
        w_message,
        w_coarse,
        w_update,
        jnp.transpose(mask_words),
        tile_index,
        partner,
        assignment,
        live_counts,
    )
    return pl.pallas_call(
        store_kernel,
        out_shape=outs,
        in_specs=[far] * 3,
        out_specs=(far,) * 3,
        scratch_shapes=[vmem(out.shape, bf16) for out in outs] + [dma((7,)), dma((7,))],
        compiler_params=pltpu.CompilerParams(vmem_limit_bytes=56 * 1024 * 1024),
        name="store",
    )(*results)


def solution(mesh):
    pieces = P(("grp", "dom", "lvl", "sub"), None)
    flat = P(("grp", "dom", "lvl", "sub"))
    return jax.shard_map(
        functools.partial(on_device, mesh.shape["dom"], mesh.shape["lvl"]),
        mesh=mesh,
        in_specs=(
            pieces,
            pieces,
            pieces,
            P(),
            P(),
            P(),
            pieces,
            pieces,
            P("grp", None),
            flat,
            flat,
        ),
        out_specs=(pieces, pieces, pieces),
        check_vma=False,
    )
```
